32 devices in a mesh: aux: 4 (over y, x), vir: 8 (over z, core).
Axes of the slice: x: 2, y: 2, z: 4, core: 2. Of those that a mesh axis runs over, the one named last changes fastest.
Arguments:
- orbitals: bfloat16 [8192, 2, 4096], P('aux', None, 'vir'), may hold values from -0.5390625 to 0.5390625
- screened: bfloat16 [8192, 8192], P('vir', 'aux'), may hold values from -0.0625 to 0.0625
- density_in: float32 [4096, 4096], P('aux', 'vir'), may hold values from -6 to 6
Outputs:
- density: float32 [4096, 4096], P('aux', 'vir')
The draws below stay inside these ranges and needn't reach their ends.
All inputs are finite; a program needn't handle non-finite values.
Results may differ from the reference program's by a relative error of at most 0.008.
Values may be sent and summed in bfloat16 or wider, within the bound.
A program may use at most 192 MiB of HBM per device.

```python
import jax
import jax.numpy as jnp
from jax import lax

V = 4096
NAUX = 8192
OCC = 2
AUX_DEV = 2048
N_AUX = 4


def levels(own_key, extent, shards, low, largest):
    def one(position, parts):
        heights = jax.random.uniform(jax.random.fold_in(jax.random.fold_in(own_key, 6), position), (parts,), jnp.float32, low / len(shards), largest / len(shards))
        return jnp.repeat(jnp.exp(heights), extent[position] // parts).reshape((-1,) + (1,) * (len(extent) - position - 1))

    loudness = one(*shards[0])
    for cut in shards[1:]:
        loudness = loudness * one(*cut)
    return loudness


def normal_values(key, extent, spread, limit, pieces=(), dtype=jnp.bfloat16):
    values = spread * jax.random.normal(key, extent, jnp.float32)
    if pieces:
        values = values * levels(key, extent, pieces, -0.22, 0.18)
    return jnp.clip(values, -limit, limit).astype(dtype)


def setup_inputs(seed: int = 0) -> dict:
    key_of = jax.random.split(jax.random.key(seed), 4)
    return {
        "orbitals": normal_values(key_of[0], (NAUX, OCC, V), 0.09, 0.5390625, ((0, 4), (2, 8))),
        "screened": normal_values(key_of[1], (NAUX, NAUX), NAUX ** -0.5, 0.0625, ((0, 8), (1, 4))),
        "density_in": normal_values(key_of[2], (V, V), 1.0, 6.0, ((0, 4), (1, 8)), jnp.float32),
    }


def reference(orbitals, screened, density_in):
    flat_orb = orbitals.reshape(NAUX, OCC * V)
    screened_orb = jnp.dot(screened.T, flat_orb, preferred_element_type=jnp.float32).astype(jnp.bfloat16)
    block_left = orbitals.reshape(N_AUX, AUX_DEV * OCC, V)
    block_right = screened_orb.reshape(N_AUX, AUX_DEV * OCC, V)

    def accumulate(running, pair):
        left_part, right_part = pair
        product = lax.dot_general(left_part, right_part, (((0,), (0,)), ((), ())), preferred_element_type=jnp.float32)
        rounded = lax.optimization_barrier(product.astype(jnp.bfloat16))
        return running + rounded.astype(jnp.float32), None

    summed, _ = lax.scan(accumulate, jnp.zeros((V, V), jnp.float32), (block_left, block_right))
    return density_in + summed
```

```python
import jax
import jax.numpy as jnp
from jax import lax
from jax.sharding import PartitionSpec as P

CORES = 2
HALVES = 2


def tie(value, other):
    if other is None:
        return value
    return lax.optimization_barrier((value, other))[0]


def dot(left, right):
    return lax.dot_general(left, right, (((0,), (0,)), ((), ())), preferred_element_type=jnp.float32).astype(jnp.bfloat16)


def make(n_aux, n_vir):
    line = n_vir // CORES
    shift = line // 4
    inner = 2 * shift
    outer_to_inner = [(g, g + shift) for g in range(shift)] + [(g, g - shift) for g in range(line - shift, line)]

    def on_cores(pairs):
        return [(a * CORES + c, b * CORES + c) for a, b in pairs for c in range(CORES)]

    hand = on_cores(outer_to_inner)
    back = [(b, a) for a, b in hand]
    swap = [(v, v ^ 1) for v in range(shift * CORES, (line - shift) * CORES)]

    def turn(r):
        return on_cores([(shift + j, shift + (j + r) % inner) for j in range(inner)])

    def shards(orbitals, screened, density_in):
        rows, occ, cols = orbitals.shape
        part = cols // HALVES
        v = lax.axis_index("vir")
        g, c = v // CORES, v % CORES
        is_inner = (g >= shift) & (g < line - shift)
        partner = jnp.where(g < line // 2, g - shift, g + shift)

        by_occ = jnp.transpose(orbitals, (1, 0, 2))
        halves = [by_occ[:, :, h * part : (h + 1) * part].reshape(occ * rows, part) for h in range(HALVES)]

        out_w = lax.ppermute(screened, "vir", hand)
        out_halves = []
        last = out_w
        for h in range(HALVES):
            last = lax.ppermute(tie(halves[h], last), "vir", hand)
            out_halves.append(last)

        flight = [None, None]

        def rotate(value, r):
            got = lax.ppermute(tie(value, flight[-2]), "vir", turn(r))
            flight.append(got)
            return got

        def source(r):
            own = shift + lax.rem(g - shift - r + 2 * inner, inner)
            return own, jnp.where(own < line // 2, own - shift, own + shift)

        w_pieces = [(g, screened), (partner, out_w)]
        for r in range(1, inner):
            own, far = source(r)
            w_pieces.append((own, rotate(screened, r)))
            w_pieces.append((far, rotate(out_w, r)))
        b_pieces = []
        for h in range(HALVES):
            b_pieces.append([(g, halves[h]), (partner, out_halves[h])])
            for r in range(1, inner):
                own, far = source(r)
                b_pieces[h].append((own, rotate(halves[h], r)))
                b_pieces[h].append((far, rotate(out_halves[h], r)))

        depth = screened.shape[0]
        w_all = jnp.zeros((depth * n_vir, screened.shape[1]), screened.dtype)
        for place, piece in w_pieces:
            other = lax.ppermute(piece, "vir", swap)
            w_all = lax.dynamic_update_slice(w_all, piece, ((place * CORES + c) * depth, 0))
            w_all = lax.dynamic_update_slice(w_all, other, ((place * CORES + 1 - c) * depth, 0))

        def screen(col_halves):
            return jnp.concatenate(
                [
                    dot(
                        w_all,
                        lax.all_gather(
                            jnp.concatenate([x[i * rows : (i + 1) * rows] for x in col_halves], axis=1),
                            "aux",
                            axis=0,
                            tiled=True,
                        ),
                    )
                    for i in range(occ)
                ],
                axis=0,
            )

        right = [screen(halves), screen(out_halves)]

        summed = [[], []]
        for h in range(HALVES):
            left = [(place * CORES + c, piece) for place, piece in b_pieces[h]]
            left += [(place * CORES + 1 - c, lax.ppermute(piece, "vir", swap)) for place, piece in b_pieces[h]]
            for side in (1, 0):
                tiles = jnp.zeros((n_vir, part, cols), jnp.bfloat16)
                for place, piece in left:
                    tiles = lax.dynamic_update_slice(tiles, dot(piece, right[side])[None], (place, 0, 0))
                mine = lax.psum_scatter(tiles, "aux", scatter_dimension=0, tiled=True)
                if side == 1:
                    mine = lax.ppermute(mine, "vir", back)
                summed[side].append(mine)
        total = [jnp.stack(x, axis=1).reshape(density_in.shape) for x in summed]
        return density_in + jnp.where(is_inner, total[0], total[1]).astype(jnp.float32)

    return shards


def solution(mesh):
    return jax.shard_map(
        make(mesh.shape["aux"], mesh.shape["vir"]),
        mesh=mesh,
        in_specs=(P("aux", None, "vir"), P("vir", "aux"), P("aux", "vir")),
        out_specs=P("aux", "vir"),
        check_vma=False,
    )
```

```python
import jax
import jax.numpy as jnp
from jax import lax
from jax.sharding import PartitionSpec as P

CORES = 2
HALVES = 2


def tie(value, other):
    if other is None:
        return value
    return lax.optimization_barrier((value, other))[0]


def dot(left, right):
    return lax.dot_general(left, right, (((0,), (0,)), ((), ())), preferred_element_type=jnp.float32).astype(jnp.bfloat16)


def make(n_aux, n_vir):
    line = n_vir // CORES
    shift = line // 4
    inner = 2 * shift
    outer_to_inner = [(g, g + shift) for g in range(shift)] + [(g, g - shift) for g in range(line - shift, line)]

    def on_cores(pairs):
        return [(a * CORES + c, b * CORES + c) for a, b in pairs for c in range(CORES)]

    hand = on_cores(outer_to_inner)
    back = [(b, a) for a, b in hand]
    swap = [(v, v ^ 1) for v in range(shift * CORES, (line - shift) * CORES)]

    def turn(r):
        return on_cores([(shift + j, shift + (j + r) % inner) for j in range(inner)])

    def shards(orbitals, screened, density_in):
        rows, occ, cols = orbitals.shape
        part = cols // HALVES
        v = lax.axis_index("vir")
        g, c = v // CORES, v % CORES
        is_inner = (g >= shift) & (g < line - shift)
        partner = jnp.where(g < line // 2, g - shift, g + shift)

        by_occ = jnp.transpose(orbitals, (1, 0, 2))
        halves = [by_occ[:, :, h * part : (h + 1) * part].reshape(occ * rows, part) for h in range(HALVES)]

        out_w = lax.ppermute(screened, "vir", hand)
        out_halves = []
        last = out_w
        for h in range(HALVES):
            last = lax.ppermute(tie(halves[h], last), "vir", hand)
            out_halves.append(last)

        def gather(block):
            return lax.all_gather(block, "aux", axis=0, tiled=True)

        own_rows = [gather(by_occ[0])]
        for i in range(1, occ):
            own_rows.append(gather(tie(by_occ[i], own_rows[-1])))
        out_rows = []
        for i in range(occ):
            block = jnp.concatenate([x[i * rows : (i + 1) * rows] for x in out_halves], axis=1)
            out_rows.append(gather(tie(block, out_rows[-1] if out_rows else own_rows[-1])))

        def source(r):
            own = shift + lax.rem(g - shift - r + 2 * inner, inner)
            return own, jnp.where(own < line // 2, own - shift, own + shift)

        flight = []

        def rotate(value, r, after):
            value = tie(value, flight[-1] if flight else None)
            flight.append(lax.ppermute(tie(value, after), "vir", turn(r)))
            return flight[-1]

        turns = range(1, inner)
        w_pieces = [(g, screened), (partner, out_w)]
        w_pieces += [(source(r)[0], rotate(screened, r, None)) for r in turns]
        w_pieces += [(source(r)[1], rotate(out_w, r, own_rows[0])) for r in turns]
        b_pieces = [[(g, halves[h]), (partner, out_halves[h])] for h in range(HALVES)]
        for h in range(HALVES):
            b_pieces[h] += [(source(r)[0], rotate(halves[h], r, own_rows[-1])) for r in turns]
        for h in range(HALVES):
            b_pieces[h] += [(source(r)[1], rotate(out_halves[h], r, out_rows[0])) for r in turns]

        depth = screened.shape[0]
        w_all = jnp.zeros((depth * n_vir, screened.shape[1]), screened.dtype)
        for place, piece in w_pieces:
            other = lax.ppermute(piece, "vir", swap)
            w_all = lax.dynamic_update_slice(w_all, piece, ((place * CORES + c) * depth, 0))
            w_all = lax.dynamic_update_slice(w_all, other, ((place * CORES + 1 - c) * depth, 0))

        right = [jnp.concatenate([dot(w_all, x) for x in side], axis=0) for side in (own_rows, out_rows)]

        left = []
        for h in range(HALVES):
            block = jnp.zeros((occ * rows, n_vir * part), orbitals.dtype)
            for place, piece in b_pieces[h]:
                other = lax.ppermute(piece, "vir", swap)
                block = lax.dynamic_update_slice(block, piece, (0, (place * CORES + c) * part))
                block = lax.dynamic_update_slice(block, other, (0, (place * CORES + 1 - c) * part))
            left.append(block)

        summed = [[], []]
        for side in (1, 0):
            for h in range(HALVES):
                mine = lax.psum_scatter(dot(left[h], right[side]), "aux", scatter_dimension=0, tiled=True)
                if side == 1:
                    mine = lax.ppermute(mine, "vir", back)
                summed[side].append(mine.reshape(-1, part, cols))
        total = [jnp.stack(x, axis=1).reshape(density_in.shape) for x in summed]
        return density_in + jnp.where(is_inner, total[0], total[1]).astype(jnp.float32)

    return shards


def solution(mesh):
    return jax.shard_map(
        make(mesh.shape["aux"], mesh.shape["vir"]),
        mesh=mesh,
        in_specs=(P("aux", None, "vir"), P("vir", "aux"), P("aux", "vir")),
        out_specs=P("aux", "vir"),
        check_vma=False,
    )
```
